1024 devices in a mesh: wide: 64 (over x, z_lo, core), narrow: 16 (over y, z_hi).
Axes of the slice: x: 4, y: 8, z: 16 (z_hi: 2, z_lo: 8; z = z_hi * 8 + z_lo), core: 2. Of those that a mesh axis runs over, the one named last changes fastest.
Arguments:
- activations: bfloat16 [131072, 4096], P(('wide', 'narrow')), may hold values from -6 to 6
- codes: bfloat16 [1024, 4, 512], P('narrow'), may hold values from -0.09375 to 0.09375
- scales: float32 [1024], P('narrow'), may hold values from 0.4 to 4
- cotangent: bfloat16 [131072, 512], P(('wide', 'narrow')), may hold values from -24 to 24
Outputs:
- values: bfloat16 [131072, 512], P(('wide', 'narrow'))
- input_grad: bfloat16 [131072, 4096], P(('wide', 'narrow'))
- weight_grad: float32 [4096, 512], P('narrow', 'wide')
The draws below stay inside these ranges and needn't reach their ends.
All inputs are finite; a program needn't handle non-finite values.
Results may differ from the reference program's by a relative error of at most 0.017.
Values may be sent and summed in bfloat16 or wider, within the bound.
No kernel may reach another device: no remote copies, remote signals or barrier semaphores. Data moves between devices by JAX's collectives and lax.ppermute only.
A program may use at most 32 MiB of HBM per device.

```python
import math
import jax
import jax.numpy as jnp
from jax import lax

DW = 4096
KVW = 512
TOK_DEV = 128
RB = 4
BLOCKS = 1024
TOKENS = 131072


def raised(values, rng, source, target, blocks, factor):
    def block_of(axis_at):
        return (jnp.arange(values.shape[axis_at]) // (values.shape[axis_at] // blocks)).reshape((-1,) + (1,) * (values.ndim - 1 - axis_at))

    near = jax.random.permutation(rng, blocks)[block_of(target)]
    other_side = (block_of(target) + blocks // 2) % blocks
    return jnp.where((block_of(source) == near) | (block_of(source) == other_side), factor * values, values)


def levels(own_key, dims, cuts, least, top_value):
    def one(position, shards_of):
        heights = jax.random.uniform(jax.random.fold_in(jax.random.fold_in(own_key, 6), position), (shards_of,), jnp.float32, least / len(cuts), top_value / len(cuts))
        return jnp.repeat(jnp.exp(heights), dims[position] // shards_of).reshape((-1,) + (1,) * (len(dims) - position - 1))

    gain = one(*cuts[0])
    for cut in cuts[1:]:
        gain = gain * one(*cut)
    return gain


def noise(key, extent, spread, bound, cuts=(), dtype=jnp.bfloat16):
    drawn = spread * jax.random.normal(key, extent, jnp.float32)
    if cuts:
        drawn = drawn * levels(key, extent, cuts, -0.22, 0.18)
    return jnp.clip(drawn, -bound, bound).astype(dtype)


def noise_with(stream_key, dims, spread, most, pieces, heavy, held_as=jnp.bfloat16):
    entries = spread * jax.random.normal(stream_key, dims, jnp.float32)
    if pieces:
        entries = entries * levels(stream_key, dims, pieces, -0.22, 0.18)
    return jnp.clip(raised(entries, jax.random.fold_in(stream_key, 3), *heavy), -most, most).astype(held_as)


def setup_inputs(seed: int = 0) -> dict:
    arg_keys = jax.random.split(jax.random.key(seed), 5)
    return {
        "activations": noise(arg_keys[0], (TOKENS, DW), 1.0, 6.0, ((0, 1024),)),
        "codes": noise(arg_keys[1], (BLOCKS, RB, KVW), DW ** -0.5, 0.09375, ((0, 16),)),
        "scales": jnp.clip(jnp.exp(math.log(4.0) - 2.3025851 * jax.random.uniform(arg_keys[2], (BLOCKS,), jnp.float32) ** levels(arg_keys[2], (BLOCKS,), ((0, 16),), -0.2, 0.2)), 0.4, 4.0),
        "cotangent": noise_with(arg_keys[3], (TOKENS, KVW), 1.0, 24.0, ((0, 1024),), (0, 1, 512, 6.0)),
    }


def reference(activations, codes, scales, cotangent):
    dense = (codes.astype(jnp.float32) * scales[:, None, None]).astype(jnp.bfloat16).reshape(DW, KVW)
    values = jnp.dot(activations, dense, preferred_element_type=jnp.float32).astype(jnp.bfloat16)
    input_grad = lax.dot_general(cotangent, dense, (((1,), (1,)), ((), ())), preferred_element_type=jnp.float32).astype(jnp.bfloat16)
    factor = 1.0 / math.sqrt(TOKENS)
    count = TOKENS // TOK_DEV
    act_blocks = activations.reshape(count, TOK_DEV, DW)
    cot_blocks = cotangent.reshape(count, TOK_DEV, KVW)

    def add_term(total, pair):
        part_act, part_cot = pair
        term = lax.dot_general(part_act, part_cot, (((0,), (0,)), ((), ())), preferred_element_type=jnp.float32) * factor
        rounded = lax.optimization_barrier(term.astype(jnp.bfloat16))
        return (total + rounded.astype(jnp.float32), None)
    weight_grad, unused = lax.scan(add_term, jnp.zeros((DW, KVW), jnp.float32), (act_blocks, cot_blocks))
    return (values, input_grad, weight_grad)
```

```python
import math

import jax
import jax.numpy as jnp
from jax import lax
from jax.sharding import Mesh
from jax.sharding import PartitionSpec as P

AXES = ("x", "l", "c", "y", "h")
Z = ("h", "l")
SIZES = (4, 8, 2, 8, 2)


def dot(a, b, contract):
    return lax.dot_general(a, b, ((contract[:1], contract[1:]), ((), ())), preferred_element_type=jnp.float32)


def swap(value, axis):
    return lax.ppermute(value, axis, [(0, 1), (1, 0)])


def after(value, *others):
    return lax.optimization_barrier((value, *others))[0]


def body(activations, codes, scales, cotangent, factor):
    nx, nl, nc, ny, nh = (lax.axis_size(a) for a in AXES)
    tok, dw = activations.shape
    kv = cotangent.shape[1]
    ix, ic, ih = lax.axis_index("x"), lax.axis_index("c"), lax.axis_index("h")
    cols = kv // (nx * nl * nc)
    rows = dw // (ny * nh)

    count = codes.shape[0] // (nx * nc)
    first = (ix * nc + ic) * count
    code_part = lax.dynamic_slice_in_dim(codes, first, count, 0)
    scale_part = lax.dynamic_slice_in_dim(scales, first, count, 0)
    part = (code_part.astype(jnp.float32) * scale_part[:, None, None]).astype(jnp.bfloat16)
    part = part.reshape(-1, kv)
    part_rows = part.shape[0]
    other_part = swap(part, "h")

    half = kv // nc
    out_col = lax.broadcasted_iota(jnp.int32, (kv, half), 1)
    in_col = lax.broadcasted_iota(jnp.int32, (kv, half), 0)
    base_col = out_col + (out_col // cols) * cols

    def pick(core):
        chosen = (in_col == base_col + core * cols).astype(jnp.bfloat16)
        return dot(cotangent, chosen, (1, 0)).astype(jnp.bfloat16)

    cot_give = pick(1 - ic)
    act_other = swap(activations, "c")
    cot_other = swap(cot_give, "c")
    cot_keep = pick(ic)
    term = dot(cot_keep, activations, (0, 0))
    term = ((term + dot(cot_other, act_other, (0, 0))) * factor).astype(jnp.bfloat16)

    pair = jnp.where(ih == 0, jnp.stack([part, other_part]), jnp.stack([other_part, part]))
    copies = jnp.broadcast_to(pair[None], (ny,) + pair.shape)
    column = lax.all_to_all(copies, "y", 0, 0)

    term = after(term.reshape(nx, nl * cols, dw), column)
    got = lax.all_to_all(term, "x", 0, 0)
    total = jnp.sum(got.astype(jnp.float32), 0).astype(jnp.bfloat16)

    total = total.reshape(nl * cols, ny, nh * rows).transpose(1, 0, 2)
    got = lax.all_to_all(total, "y", 0, 0)
    total = jnp.sum(got.astype(jnp.float32), 0).astype(jnp.bfloat16)

    column = after(column, got)
    mine = lax.all_to_all(jnp.broadcast_to(column[None], (nx,) + column.shape), "x", 0, 0)
    theirs = swap(mine, "c")

    total = total.reshape(nl, cols, nh, rows).transpose(2, 0, 1, 3).reshape(nh * nl, cols, rows)
    got = lax.all_to_all(total, Z, 0, 0)
    weight_grad = jnp.sum(got.astype(jnp.float32), 0).T

    pair = jnp.where(ic == 0, jnp.stack([mine, theirs]), jnp.stack([theirs, mine]))
    dense = pair.transpose(2, 3, 1, 0, 4, 5).reshape(dw, kv)
    values = dot(activations, dense, (1, 0)).astype(jnp.bfloat16)
    grad_inputs = dot(cotangent, dense, (1, 1)).astype(jnp.bfloat16)
    return values, grad_inputs, weight_grad


def solution(mesh):
    fine = Mesh(mesh.devices.reshape(SIZES), AXES)
    wide, narrow = ("x", "l", "c"), ("y", "h")
    tokens = P(AXES, None)

    def run(activations, codes, scales, cotangent):
        factor = 1.0 / math.sqrt(activations.shape[0])
        return jax.shard_map(
            lambda *args: body(*args, factor),
            mesh=fine,
            in_specs=(tokens, P(narrow, None, None), P(narrow), tokens),
            out_specs=(tokens, tokens, P(narrow, wide)),
            check_vma=False,
        )(activations, codes, scales, cotangent)

    return run
```

```python
import functools
import math

import jax
import jax.numpy as jnp
import numpy as np
from jax import lax
from jax.experimental import pallas as pl
from jax.experimental.pallas import tpu as pltpu
from jax.sharding import Mesh
from jax.sharding import PartitionSpec as P

AXES = ("x", "l", "c", "Y", "y", "h")
INTERPRET = False
SIZES = (4, 8, 2, 4, 2, 2)


def dot(a, b, contract):
    return lax.dot_general(a, b, ((contract[:1], contract[1:]), ((), ())), preferred_element_type=jnp.float32)


def swap(value, axis):
    return lax.ppermute(value, axis, [(0, 1), (1, 0)])


def after(value, *others):
    return lax.optimization_barrier((value, *others))[0]


def term_kernel(factor, keep_ref, other_ref, act_ref, act_other_ref, out_ref):
    both = dot(keep_ref[...], act_ref[...], (1, 0)) + dot(other_ref[...], act_other_ref[...], (1, 0))
    out_ref[...] = (both * factor).astype(out_ref.dtype).reshape(out_ref.shape)


def products(place, act_ref, cot_ref, mine_ref, theirs_ref, values_ref, grad_ref, dense_ref):
    ic, ih = place[0], place[1]
    ny, nh, height, _ = mine_ref.shape
    for dc, source in enumerate((mine_ref, theirs_ref)):
        c = lax.rem(ic + dc, 2)

        @pl.loop(0, ny)
        def _(y):
            for dh in range(nh):
                row = ((y * nh + lax.rem(ih + dh, nh)) * 2 + c) * height
                dense_ref[pl.ds(pl.multiple_of(row, height), height), :] = source[y, dh]

    values_ref[...] = dot(act_ref[...], dense_ref[...], (1, 0)).astype(values_ref.dtype)
    cot = cot_ref[...]
    step = min(512, dense_ref.shape[0])

    @pl.loop(0, dense_ref.shape[0] // step)
    def _(k):
        at = pl.ds(pl.multiple_of(k * step, step), step)
        grad_ref[:, at] = dot(cot, dense_ref[at, :], (1, 1)).astype(grad_ref.dtype)


def body(activations, codes, scales, cotangent, factor):
    nx, nl, nc, nY, ny, nh = (lax.axis_size(a) for a in AXES)
    tok, dw = activations.shape
    kv = cotangent.shape[1]
    ic, ih = lax.axis_index("c"), lax.axis_index("h")
    cols = kv // (nx * nl * nc)
    rows = dw // (nY * ny * nh)

    count = codes.shape[0] // nc
    first = ic * count
    code_part = lax.dynamic_slice_in_dim(codes, first, count, 0)
    scale_part = lax.dynamic_slice_in_dim(scales, first, count, 0)
    part = (code_part.astype(jnp.float32) * scale_part[:, None, None]).astype(jnp.bfloat16)
    part = part.reshape(-1, kv)

    half = kv // nc
    base = np.arange(kv, dtype=np.int32).reshape(nx * nl, nc, cols)[:, 0]
    base = base.reshape(half, 1)
    in_col = lax.broadcasted_iota(jnp.int32, (half, kv), 1)

    def pick(core):
        chosen = (in_col == base + core * cols).astype(jnp.bfloat16)
        return dot(chosen, cotangent, (1, 1)).astype(jnp.bfloat16)

    vmem = pl.BlockSpec(memory_space=pltpu.VMEM)
    act_other = swap(activations, "c")
    cot_other = swap(pick(1 - ic), "c")
    step = nh * rows
    parts = (nx, ny, nl * cols, nY * step)
    term = pl.pallas_call(
        functools.partial(term_kernel, factor),
        out_shape=jax.ShapeDtypeStruct(parts, jnp.bfloat16),
        grid=(dw // step,),
        in_specs=[pl.BlockSpec((half, tok), lambda k: (0, 0))] * 2 + [pl.BlockSpec((tok, step), lambda k: (0, k))] * 2,
        out_specs=pl.BlockSpec((nx, 1, nl * cols, step), lambda k: (0, k % ny, 0, k // ny)),
        compiler_params=pltpu.CompilerParams(vmem_limit_bytes=16 * 2**20),
        cost_estimate=pl.CostEstimate(flops=4 * tok * dw * half, bytes_accessed=8 * tok * dw, transcendentals=0),
        interpret=INTERPRET,
    )(pick(ic), cot_other, activations, act_other)

    pair = jnp.concatenate([part, swap(part, "h")])
    mine = lax.all_gather(pair, ("Y", "y"), axis=0, tiled=True)

    got = lax.all_to_all(term.reshape(nx * ny, *parts[2:]), ("x", "y"), 0, 0)
    total = jnp.sum(got.astype(jnp.float32), 0).astype(jnp.bfloat16)

    total = total.reshape(nl * cols, nY, step).transpose(1, 0, 2)
    got = lax.all_to_all(total, "Y", 0, 0)
    total = jnp.sum(got.astype(jnp.float32), 0).astype(jnp.bfloat16)

    total = total.reshape(nl, cols, nh, rows).transpose(2, 0, 1, 3).reshape(nh * nl, cols, rows)
    got = lax.all_to_all(total, ("h", "l"), 0, 0)
    weight_grad = jnp.sum(got.astype(jnp.float32), 0).T

    mine = after(mine, got)
    theirs = swap(mine, "c")

    place = jnp.stack([ic, ih]).astype(jnp.int32)
    blocks = (nY * ny, nh, part.shape[0], kv)
    values, grad_inputs = pl.pallas_call(
        products,
        out_shape=(
            jax.ShapeDtypeStruct((tok, kv), jnp.bfloat16),
            jax.ShapeDtypeStruct((tok, dw), jnp.bfloat16),
        ),
        in_specs=[pl.BlockSpec(memory_space=pltpu.SMEM), vmem, vmem, vmem, vmem],
        out_specs=(vmem, vmem),
        scratch_shapes=[pltpu.VMEM((dw, kv), jnp.bfloat16)],
        compiler_params=pltpu.CompilerParams(vmem_limit_bytes=24 * 2**20),
        cost_estimate=pl.CostEstimate(flops=4 * tok * dw * kv, bytes_accessed=4 * dw * kv, transcendentals=0),
        interpret=INTERPRET,
    )(place, activations, cotangent, mine.reshape(blocks), theirs.reshape(blocks))
    return values, grad_inputs, weight_grad


def solution(mesh):
    fine = Mesh(mesh.devices.reshape(SIZES), AXES)
    wide, narrow = AXES[:3], AXES[3:]
    tokens = P(AXES, None)

    def run(activations, codes, scales, cotangent):
        factor = 1.0 / math.sqrt(activations.shape[0])
        return jax.shard_map(
            lambda *args: body(*args, factor),
            mesh=fine,
            in_specs=(tokens, P(narrow, None, None), P(narrow), tokens),
            out_specs=(tokens, tokens, P(narrow, wide)),
            check_vma=False,
        )(activations, codes, scales, cotangent)

    return run
```

```python
import functools
import math

import jax
import jax.numpy as jnp
import numpy as np
from jax import lax
from jax.experimental import pallas as pl
from jax.experimental.pallas import tpu as pltpu
from jax.sharding import Mesh
from jax.sharding import PartitionSpec as P

AXES = ("x", "l", "c", "Y", "y", "h")
INTERPRET = False
SIZES = (4, 8, 2, 4, 2, 2)


def dot(a, b, contract):
    return lax.dot_general(a, b, ((contract[:1], contract[1:]), ((), ())), preferred_element_type=jnp.float32)


def swap(value, axis):
    return lax.ppermute(value, axis, [(0, 1), (1, 0)])


def after(value, *others):
    return lax.optimization_barrier((value, *others))[0]


def term_kernel(factor, keep_ref, other_ref, act_ref, act_other_ref, out_ref):
    both = dot(keep_ref[...], act_ref[...], (1, 0)) + dot(other_ref[...], act_other_ref[...], (1, 0))
    out_ref[...] = (both * factor).astype(out_ref.dtype).reshape(out_ref.shape)


def half_products(core, place, act_ref, cot_ref, dense_ref, held_ref):
    ny, nh, height, kv = dense_ref.shape
    c = lax.rem(place[0] + core, 2)

    def column(y, dh):
        start = ((y * nh + lax.rem(place[1] + dh, nh)) * 2 + c) * height
        return pl.ds(pl.multiple_of(start, height), height)

    for y in range(ny):
        for dh in range(nh):
            held_ref[:, pl.ds((y * nh + dh) * height, height)] = act_ref[:, column(y, dh)]
    total = dot(held_ref[...], dense_ref[...].reshape(ny * nh * height, kv), (1, 0))

    def grad(y):
        return dot(cot_ref[...], dense_ref[y].reshape(nh * height, kv), (1, 1)).astype(jnp.bfloat16)

    return total, grad, column


def own_kernel(place, act_ref, cot_ref, mine_ref, sum_ref, grad_ref, held_ref):
    total, grad, _ = half_products(0, place, act_ref, cot_ref, mine_ref, held_ref)
    sum_ref[...] = total
    for y in range(mine_ref.shape[0]):
        grad_ref[y] = grad(y)


def other_kernel(place, act_ref, cot_ref, theirs_ref, sum_ref, own_ref, values_ref, grad_ref, held_ref):
    total, grad, column = half_products(1, place, act_ref, cot_ref, theirs_ref, held_ref)
    values_ref[...] = (total + sum_ref[...]).astype(values_ref.dtype)
    ny, nh, height, _ = theirs_ref.shape
    for y in range(ny):
        piece = grad(y)
        for dh in range(nh):
            at = pl.ds(dh * height, height)
            other = column(y, dh)
            grad_ref[:, other] = piece[:, dh * height : (dh + 1) * height]
            c = lax.rem(place[0], 2)
            start = ((y * nh + lax.rem(place[1] + dh, nh)) * 2 + c) * height
            grad_ref[:, pl.ds(pl.multiple_of(start, height), height)] = own_ref[y, :, at]


def body(activations, codes, scales, cotangent, factor):
    nx, nl, nc, nY, ny, nh = (lax.axis_size(a) for a in AXES)
    tok, dw = activations.shape
    kv = cotangent.shape[1]
    ic, ih = lax.axis_index("c"), lax.axis_index("h")
    cols = kv // (nx * nl * nc)
    rows = dw // (nY * ny * nh)

    count = codes.shape[0] // nc
    first = ic * count
    code_part = lax.dynamic_slice_in_dim(codes, first, count, 0)
    scale_part = lax.dynamic_slice_in_dim(scales, first, count, 0)
    part = (code_part.astype(jnp.float32) * scale_part[:, None, None]).astype(jnp.bfloat16)
    part = part.reshape(-1, kv)

    half = kv // nc
    base = np.arange(kv, dtype=np.int32).reshape(nx * nl, nc, cols)[:, 0]
    base = base.reshape(half, 1)
    in_col = lax.broadcasted_iota(jnp.int32, (half, kv), 1)

    def pick(core):
        chosen = (in_col == base + core * cols).astype(jnp.bfloat16)
        return dot(chosen, cotangent, (1, 1)).astype(jnp.bfloat16)

    vmem = pl.BlockSpec(memory_space=pltpu.VMEM)
    act_other = swap(activations, "c")
    cot_other = swap(pick(1 - ic), "c")
    step = nh * rows
    parts = (nx, ny, nl * cols, nY * step)
    term = pl.pallas_call(
        functools.partial(term_kernel, factor),
        out_shape=jax.ShapeDtypeStruct(parts, jnp.bfloat16),
        grid=(dw // step,),
        in_specs=[pl.BlockSpec((half, tok), lambda k: (0, 0))] * 2 + [pl.BlockSpec((tok, step), lambda k: (0, k))] * 2,
        out_specs=pl.BlockSpec((nx, 1, nl * cols, step), lambda k: (0, k % ny, 0, k // ny)),
        compiler_params=pltpu.CompilerParams(vmem_limit_bytes=16 * 2**20),
        cost_estimate=pl.CostEstimate(flops=4 * tok * dw * half, bytes_accessed=8 * tok * dw, transcendentals=0),
        interpret=INTERPRET,
    )(pick(ic), cot_other, activations, act_other)

    pair = jnp.concatenate([part, swap(part, "h")])
    mine = lax.all_gather(pair, ("Y", "y"), axis=0, tiled=True)

    got = lax.all_to_all(term.reshape(nx * ny, *parts[2:]), ("x", "y"), 0, 0)
    total = jnp.sum(got.astype(jnp.float32), 0).astype(jnp.bfloat16)

    total = total.reshape(nl * cols, nY, step).transpose(1, 0, 2)
    got = lax.all_to_all(total, "Y", 0, 0)
    total = jnp.sum(got.astype(jnp.float32), 0).astype(jnp.bfloat16)

    total = total.reshape(nl, cols, nh, rows).transpose(2, 0, 1, 3).reshape(nh * nl, cols, rows)
    got = lax.all_to_all(total, ("h", "l"), 0, 0)
    weight_grad = jnp.sum(got.astype(jnp.float32), 0).T

    mine = after(mine, got)
    theirs = swap(mine, "c")

    place = jnp.stack([ic, ih]).astype(jnp.int32)
    blocks = (nY * ny, nh, part.shape[0], kv)
    smem = pl.BlockSpec(memory_space=pltpu.SMEM)
    width = dw // nc

    def kernel(body, outs, operands):
        return pl.pallas_call(
            body,
            out_shape=tuple(jax.ShapeDtypeStruct(*out) for out in outs),
            in_specs=[smem] + [vmem] * len(operands),
            out_specs=(vmem, vmem),
            scratch_shapes=[pltpu.VMEM((tok, width), jnp.bfloat16)],
            compiler_params=pltpu.CompilerParams(vmem_limit_bytes=24 * 2**20),
            cost_estimate=pl.CostEstimate(flops=2 * tok * dw * kv, bytes_accessed=2 * dw * kv, transcendentals=0),
            interpret=INTERPRET,
        )(place, *operands)

    own_sum, own_grad = kernel(
        own_kernel,
        [((tok, kv), jnp.float32), ((blocks[0], tok, width // blocks[0]), jnp.bfloat16)],
        (activations, cotangent, mine.reshape(blocks)),
    )
    values, grad_inputs = kernel(
        other_kernel,
        [((tok, kv), jnp.bfloat16), ((tok, dw), jnp.bfloat16)],
        (activations, cotangent, theirs.reshape(blocks), own_sum, own_grad),
    )
    return values, grad_inputs, weight_grad


def solution(mesh):
    fine = Mesh(mesh.devices.reshape(SIZES), AXES)
    wide, narrow = AXES[:3], AXES[3:]
    tokens = P(AXES, None)

    def run(activations, codes, scales, cotangent):
        factor = 1.0 / math.sqrt(activations.shape[0])
        return jax.shard_map(
            lambda *args: body(*args, factor),
            mesh=fine,
            in_specs=(tokens, P(narrow, None, None), P(narrow), tokens),
            out_specs=(tokens, tokens, P(narrow, wide)),
            check_vma=False,
        )(activations, codes, scales, cotangent)

    return run
```

```python
import functools
import math

import jax
import jax.numpy as jnp
import numpy as np
from jax import lax
from jax.experimental import pallas as pl
from jax.experimental.pallas import tpu as pltpu
from jax.sharding import Mesh
from jax.sharding import PartitionSpec as P

AXES = ("x", "l", "c", "Y", "y", "h")
INTERPRET = False
SIZES = (4, 8, 2, 4, 2, 2)


def dot(a, b, contract):
    return lax.dot_general(a, b, ((contract[:1], contract[1:]), ((), ())), preferred_element_type=jnp.float32)


def swap(value, axis):
    return lax.ppermute(value, axis, [(0, 1), (1, 0)])


def after(value, *others):
    return lax.optimization_barrier((value, *others))[0]


def term_kernel(factor, step, keep_ref, other_ref, act_ref, act_other_ref, out_ref):
    nx, ny, height, width = out_ref.shape
    for k in range(act_ref.shape[1] // step):
        at = pl.ds(k * step, step)
        both = dot(keep_ref[...], act_ref[:, at], (1, 0)) + dot(other_ref[...], act_other_ref[:, at], (1, 0))
        piece = (both * factor).astype(out_ref.dtype).reshape(nx, height, step)
        out_ref[:, k % ny, :, pl.ds(k // ny * step, step)] = piece


def half_products(core, place, act_ref, cot_ref, dense_ref, held_ref):
    ny, nh, height, kv = dense_ref.shape
    c = lax.rem(place[0] + core, 2)

    def column(y, dh):
        start = ((y * nh + lax.rem(place[1] + dh, nh)) * 2 + c) * height
        return pl.ds(pl.multiple_of(start, height), height)

    for y in range(ny):
        for dh in range(nh):
            held_ref[:, pl.ds((y * nh + dh) * height, height)] = act_ref[:, column(y, dh)]
    total = dot(held_ref[...], dense_ref[...].reshape(ny * nh * height, kv), (1, 0))

    def grad(y):
        return dot(cot_ref[...], dense_ref[y].reshape(nh * height, kv), (1, 1)).astype(jnp.bfloat16)

    return total, grad, column


def own_kernel(place, act_ref, cot_ref, mine_ref, sum_ref, grad_ref, held_ref):
    total, grad, _ = half_products(0, place, act_ref, cot_ref, mine_ref, held_ref)
    sum_ref[...] = total
    for y in range(mine_ref.shape[0]):
        grad_ref[y] = grad(y)


def other_kernel(place, act_ref, cot_ref, theirs_ref, sum_ref, own_ref, values_ref, grad_ref, held_ref):
    total, grad, column = half_products(1, place, act_ref, cot_ref, theirs_ref, held_ref)
    values_ref[...] = (total + sum_ref[...]).astype(values_ref.dtype)
    ny, nh, height, _ = theirs_ref.shape
    for y in range(ny):
        piece = grad(y)
        for dh in range(nh):
            at = pl.ds(dh * height, height)
            other = column(y, dh)
            grad_ref[:, other] = piece[:, dh * height : (dh + 1) * height]
            c = lax.rem(place[0], 2)
            start = ((y * nh + lax.rem(place[1] + dh, nh)) * 2 + c) * height
            grad_ref[:, pl.ds(pl.multiple_of(start, height), height)] = own_ref[y, :, at]


def body(activations, codes, scales, cotangent, factor):
    nx, nl, nc, nY, ny, nh = (lax.axis_size(a) for a in AXES)
    tok, dw = activations.shape
    kv = cotangent.shape[1]
    ic, ih = lax.axis_index("c"), lax.axis_index("h")
    cols = kv // (nx * nl * nc)
    rows = dw // (nY * ny * nh)

    count = codes.shape[0] // nc
    first = ic * count
    code_part = lax.dynamic_slice_in_dim(codes, first, count, 0)
    scale_part = lax.dynamic_slice_in_dim(scales, first, count, 0)
    part = (code_part.astype(jnp.float32) * scale_part[:, None, None]).astype(jnp.bfloat16)
    part = part.reshape(-1, kv)

    half = kv // nc
    base = np.arange(kv, dtype=np.int32).reshape(nx * nl, nc, cols)[:, 0]
    base = base.reshape(half, 1)
    in_col = lax.broadcasted_iota(jnp.int32, (half, kv), 1)

    def pick(core):
        chosen = (in_col == base + core * cols).astype(jnp.bfloat16)
        return dot(chosen, cotangent, (1, 1)).astype(jnp.bfloat16)

    vmem = pl.BlockSpec(memory_space=pltpu.VMEM)
    act_other = swap(activations, "c")
    cot_other = swap(pick(1 - ic), "c")
    step = nh * rows
    parts = (nx, ny, nl * cols, nY * step)
    term = pl.pallas_call(
        functools.partial(term_kernel, factor, step),
        out_shape=jax.ShapeDtypeStruct(parts, jnp.bfloat16),
        in_specs=[vmem] * 4,
        out_specs=vmem,
        compiler_params=pltpu.CompilerParams(vmem_limit_bytes=16 * 2**20),
        cost_estimate=pl.CostEstimate(flops=4 * tok * dw * half, bytes_accessed=8 * tok * dw, transcendentals=0),
        interpret=INTERPRET,
    )(pick(ic), cot_other, activations, act_other)

    pair = jnp.concatenate([part, swap(part, "h")])
    mine = lax.all_gather(pair, ("Y", "y"), axis=0, tiled=True)

    got = lax.all_to_all(term.reshape(nx * ny, *parts[2:]), ("x", "y"), 0, 0)
    total = jnp.sum(got.astype(jnp.float32), 0).astype(jnp.bfloat16)

    total = total.reshape(nl * cols, nY, step).transpose(1, 0, 2)
    got = lax.all_to_all(total, "Y", 0, 0)
    total = jnp.sum(got.astype(jnp.float32), 0).astype(jnp.bfloat16)

    total = total.reshape(nl, cols, nh, rows).transpose(2, 0, 1, 3).reshape(nh * nl, cols, rows)
    got = lax.all_to_all(total, ("h", "l"), 0, 0)
    weight_grad = jnp.sum(got.astype(jnp.float32), 0).T

    mine = after(mine, got)
    theirs = swap(mine, "c")

    place = jnp.stack([ic, ih]).astype(jnp.int32)
    blocks = (nY * ny, nh, part.shape[0], kv)
    smem = pl.BlockSpec(memory_space=pltpu.SMEM)
    width = dw // nc

    def kernel(body, outs, operands):
        return pl.pallas_call(
            body,
            out_shape=tuple(jax.ShapeDtypeStruct(*out) for out in outs),
            in_specs=[smem] + [vmem] * len(operands),
            out_specs=(vmem, vmem),
            scratch_shapes=[pltpu.VMEM((tok, width), jnp.bfloat16)],
            compiler_params=pltpu.CompilerParams(vmem_limit_bytes=24 * 2**20),
            cost_estimate=pl.CostEstimate(flops=2 * tok * dw * kv, bytes_accessed=2 * dw * kv, transcendentals=0),
            interpret=INTERPRET,
        )(place, *operands)

    own_sum, own_grad = kernel(
        own_kernel,
        [((tok, kv), jnp.float32), ((blocks[0], tok, width // blocks[0]), jnp.bfloat16)],
        (activations, cotangent, mine.reshape(blocks)),
    )
    values, grad_inputs = kernel(
        other_kernel,
        [((tok, kv), jnp.bfloat16), ((tok, dw), jnp.bfloat16)],
        (activations, cotangent, theirs.reshape(blocks), own_sum, own_grad),
    )
    return values, grad_inputs, weight_grad


def solution(mesh):
    fine = Mesh(mesh.devices.reshape(SIZES), AXES)
    wide, narrow = AXES[:3], AXES[3:]
    tokens = P(AXES, None)

    def run(activations, codes, scales, cotangent):
        factor = 1.0 / math.sqrt(activations.shape[0])
        return jax.shard_map(
            lambda *args: body(*args, factor),
            mesh=fine,
            in_specs=(tokens, P(narrow, None, None), P(narrow), tokens),
            out_specs=(tokens, tokens, P(narrow, wide)),
            check_vma=False,
        )(activations, codes, scales, cotangent)

    return run
```
